32 devices in a mesh: station: 8 (over y, x, core), section: 4 (over z).
Axes of the slice: x: 2, y: 2, z: 4, core: 2. Of those that a mesh axis runs over, the one named last changes fastest.
Arguments:
- voltages: bfloat16 [8, 128, 17408], P('station', 'section'), may hold values from -6 to 6
- taper: float32 [14, 1024], replicated, may hold values from -1.6 to 1.6
- beam_weight_table: bfloat16 [8, 8, 128, 2, 512], P('station', None, 'section'), may hold values from -1 to 1
- starts: int32 [8], replicated, may hold values from 0 to 3
- owner_map: int32 [512], replicated, may hold values from 0 to 7, as said below
Outputs:
- visibilities: bfloat16 [4, 8, 16, 8, 4, 16, 32], P('section', 'station')
The draws below stay inside these ranges and needn't reach their ends.
Inputs may be any that keep to these rules, and one draw needn't show every extreme that they name: `owner_map`: within each block of 128 consecutive channels every owner 0 to 7 owns exactly 16 channels.
All inputs are finite; a program needn't handle non-finite values.
Results may differ from the reference program's by a relative error of at most 0.014.
Values may be sent and summed in bfloat16 or wider, within the bound.
A program may use at most 64 MiB of HBM per device.

```python
import math
import jax
import jax.numpy as jnp
from jax import lax

NFFT = 1024
TAPS = 14
BEAM_TOTAL = 8
SECTION_ANTENNAS = 16
FRAMES = 4
FREQ_CHANNELS = 512
STATION_SECTIONS = 4
ARRAY_STATIONS = 8
STATION_ANTENNAS = 64
SIGNAL_INPUTS = 128
SAMPLES = 17408
SPAN = 2
CPO = 16


def draw_owner_map(key, part):
    block = FREQ_CHANNELS // STATION_SECTIONS
    several = jax.random.split(key, STATION_SECTIONS)
    orders = jax.vmap(lambda single: jax.random.permutation(single, block))(several)
    return (orders // CPO).reshape(FREQ_CHANNELS).astype(jnp.int32)


def set_ends(drawn, stream_key, smallest, top_value):
    longest = drawn.shape.index(max(drawn.shape))
    spots = []
    for shift in (0, 1):
        where = [jax.random.randint(jax.random.fold_in(stream_key, axis), (), 0, length) for axis, length in enumerate(drawn.shape)]
        where[longest] = (where[longest] + shift) % drawn.shape[longest]
        spots.append(tuple(where))
    return drawn.at[spots[0]].set(smallest).at[spots[1]].set(top_value)


def steps_of(own_key, shape, pieces, smallest, largest):
    gain = 1.0
    for axis_at, parts in pieces:
        heights = jax.random.uniform(jax.random.fold_in(jax.random.fold_in(own_key, 6), axis_at), (parts,), jnp.float32, smallest / len(pieces), largest / len(pieces))
        gain = gain * jnp.repeat(jnp.exp(heights), shape[axis_at] // parts).reshape((-1,) + (1,) * (len(shape) - 1 - axis_at))
    return gain


def gaussian(rng, dims, scale, bound, cuts=(), kind=jnp.bfloat16):
    array = scale * jax.random.normal(rng, dims, jnp.float32)
    if cuts:
        array = array * steps_of(rng, dims, cuts, -0.22, 0.18)
    return jnp.clip(array, -bound, bound).astype(kind)


def setup_inputs(seed: int = 0) -> dict:
    streams_of = jax.random.split(jax.random.key(seed), 6)
    voltages = gaussian(streams_of[0], (ARRAY_STATIONS, SIGNAL_INPUTS, SAMPLES), 1.0, 6.0, ((0, 8), (1, 4)))
    taper = gaussian(streams_of[1], (TAPS, NFFT), 0.27, 1.6, (), jnp.float32)
    beam_weight_table = gaussian(streams_of[2], (ARRAY_STATIONS, BEAM_TOTAL, SIGNAL_INPUTS, 2, FREQ_CHANNELS), (SECTION_ANTENNAS * STATION_SECTIONS // 2) ** -0.5, 1.0, ((0, 8), (2, 4)))
    starts = set_ends(jax.random.randint(streams_of[3], (BEAM_TOTAL,), 0, STATION_SECTIONS), jax.random.fold_in(streams_of[3], 1), 0, STATION_SECTIONS - 1).astype(jnp.int32)
    owner_map = draw_owner_map(jax.random.fold_in(streams_of[5], 71), 0)
    return {"voltages": voltages, "taper": taper, "beam_weight_table": beam_weight_table, "starts": starts, "owner_map": owner_map}


def dft_table():
    index_n = jnp.arange(NFFT, dtype=jnp.int32)[:, None]
    index_k = jnp.arange(FREQ_CHANNELS, dtype=jnp.int32)[None, :]
    phase = (index_n * index_k % NFFT).astype(jnp.float32) * (2.0 * math.pi / NFFT)
    factor = 1.0 / math.sqrt(NFFT)
    return jnp.concatenate([jnp.cos(phase) * factor, -jnp.sin(phase) * factor], axis=1).astype(jnp.bfloat16)

def station_beams(volts, weights, inside, taper, table):
    framed = volts.reshape(SIGNAL_INPUTS, FRAMES + TAPS - 1, NFFT)
    filtered = jnp.zeros((SIGNAL_INPUTS, FRAMES, NFFT), jnp.float32)
    for tap in range(TAPS):
        filtered = filtered + taper[tap][None, None, :] * framed[:, tap:tap + FRAMES, :].astype(jnp.float32)
    rows = filtered.astype(jnp.bfloat16).reshape(SIGNAL_INPUTS * FRAMES, NFFT)
    spectra = jnp.dot(rows, table, preferred_element_type=jnp.float32)
    spectra = spectra.reshape(STATION_ANTENNAS, 2, FRAMES, 2, FREQ_CHANNELS)
    real_x = spectra[:, :, :, 0, :]
    imag_x = spectra[:, :, :, 1, :]
    scaled = weights.astype(jnp.float32).reshape(BEAM_TOTAL, STATION_ANTENNAS, 2, 2, FREQ_CHANNELS) * inside[:, :, None, None, None]
    real_w = scaled[:, :, :, 0, :]
    imag_w = scaled[:, :, :, 1, :]
    real_b = jnp.einsum('bapk,apfk->kbpf', real_w, real_x) - jnp.einsum('bapk,apfk->kbpf', imag_w, imag_x)
    imag_b = jnp.einsum('bapk,apfk->kbpf', real_w, imag_x) + jnp.einsum('bapk,apfk->kbpf', imag_w, real_x)
    return jnp.stack([real_b, imag_b], axis=3).astype(jnp.bfloat16)

def correlate(pair):
    real_z, imag_z = pair
    real_v = jnp.einsum('bfi,bfj->bfij', real_z, real_z) + jnp.einsum('bfi,bfj->bfij', imag_z, imag_z)
    imag_v = jnp.einsum('bfi,bfj->bfij', imag_z, real_z) - jnp.einsum('bfi,bfj->bfij', real_z, imag_z)
    return jnp.concatenate([real_v, imag_v], axis=-1).astype(jnp.bfloat16)

def reference(voltages, taper, beam_weight_table, starts, owner_map):
    table = dft_table()
    section_lookup = jnp.arange(STATION_ANTENNAS, dtype=jnp.int32) // SECTION_ANTENNAS
    offset = jnp.remainder(section_lookup[None, :] - starts[:, None], STATION_SECTIONS)
    inside = (offset < SPAN).astype(jnp.float32)

    def one_station(pair):
        return station_beams(pair[0], pair[1], inside, taper, table)
    beams = lax.map(one_station, (voltages, beam_weight_table))
    block = FREQ_CHANNELS // STATION_SECTIONS
    ranked = jnp.argsort(owner_map.reshape(STATION_SECTIONS, block), axis=1, stable=True).astype(jnp.int32)
    ranked = (ranked + jnp.arange(STATION_SECTIONS, dtype=jnp.int32)[:, None] * block).reshape(FREQ_CHANNELS)
    picked = jnp.take(beams, ranked, axis=1)
    picked = jnp.transpose(picked, (1, 2, 5, 0, 3, 4)).astype(jnp.float32)
    real_z = picked[..., 0].reshape(FREQ_CHANNELS, BEAM_TOTAL, FRAMES, 2 * ARRAY_STATIONS)
    imag_z = picked[..., 1].reshape(FREQ_CHANNELS, BEAM_TOTAL, FRAMES, 2 * ARRAY_STATIONS)
    visible = lax.map(correlate, (real_z, imag_z))
    return visible.reshape(STATION_SECTIONS, ARRAY_STATIONS, CPO, BEAM_TOTAL, FRAMES, 2 * ARRAY_STATIONS, 4 * ARRAY_STATIONS)
```

```python
import functools
import math

import jax
import jax.numpy as jnp
import numpy as np
from jax import lax
from jax.experimental import pallas as pl
from jax.experimental.pallas import tpu as pltpu
from jax.sharding import PartitionSpec as P

MESH = pl.DeviceIdType.MESH
LANES = 128
F32 = jnp.float32
BF16 = jnp.bfloat16


def dft_table(length, group):
    half = length // 2
    index_n = np.arange(length, dtype=np.int64)[:, None]
    index_k = np.arange(half, dtype=np.int64)[None, :]
    phase = (index_n * index_k % length).astype(np.float32) * np.float32(2.0 * math.pi / length)
    factor = np.float32(1.0 / math.sqrt(length))
    real = (np.cos(phase) * factor).reshape(length, half // group, group)
    imag = (-np.sin(phase) * factor).reshape(length, half // group, group)
    return np.concatenate([real, imag], axis=2).transpose(1, 0, 2).astype(jnp.bfloat16)


def beam_kernel(
    dims, starts_ref, owner_ref, taper_ref, volts_hbm, weights_hbm, table_hbm, out_ref,
    volts, weights, table, filtered, spectra, outgoing, arrived, load_sems, send_sem, recv_sem,
):
    sections, stations, inputs, frames, taps, length, beams, group, block, per_owner, rows = dims
    st = lax.axis_index("station")
    sec = lax.axis_index("section")
    devices = sections * stations
    me = sec * stations + st
    groups = table.shape[0]
    group_blocks = group // block
    group_targets = group_blocks * stations

    loads = [
        pltpu.make_async_copy(volts_hbm.at[0], volts, load_sems.at[0]),
        pltpu.make_async_copy(table_hbm, table, load_sems.at[1]),
        pltpu.make_async_copy(weights_hbm, weights, load_sems.at[2]),
    ]
    for load in loads:
        load.start()

    barrier = pltpu.get_barrier_semaphore()

    def greet(step, carry):
        other = lax.rem(me + step, devices)
        pl.semaphore_signal(
            barrier, inc=1, device_id=(lax.rem(other, stations), lax.div(other, stations)),
            device_id_type=MESH,
        )
        return carry

    lax.fori_loop(1, devices, greet, 0)

    loads[0].wait()

    def filter_chunk(chunk, carry):
        at = pl.multiple_of(chunk * LANES, LANES)
        sums = [None] * frames
        for segment in range(frames + taps - 1):
            lanes = pl.ds(pl.multiple_of(segment * length + at, LANES), LANES)
            part = volts[:, lanes].astype(F32)
            for frame in range(frames):
                tap = segment - frame
                if 0 <= tap < taps:
                    term = taper_ref[tap : tap + 1, pl.ds(at, LANES)] * part
                    sums[frame] = term if sums[frame] is None else sums[frame] + term
        for frame in range(frames):
            filtered[frame * inputs : (frame + 1) * inputs, pl.ds(at, LANES)] = sums[frame].astype(BF16)
        return carry

    lax.fori_loop(0, length // LANES, filter_chunk, 0)

    beam_row = lax.broadcasted_iota(jnp.int32, (beams, group), 0)
    first = jnp.zeros((beams, group), jnp.int32)
    for beam in range(beams):
        first = jnp.where(beam_row == beam, starts_ref[beam], first)
    offset = sec - first
    offset = jnp.where(offset < 0, offset + sections, offset)
    inside = (offset < max(1, sections // 2)).astype(F32)

    def block_of(axis, shape):
        at = lax.broadcasted_iota(jnp.int32, shape, axis)
        total = jnp.zeros(shape, jnp.int32)
        for edge in range(1, group_blocks):
            total = total + (at >= edge * block).astype(jnp.int32)
        return total

    square = (group, group)
    earlier = lax.broadcasted_iota(jnp.int32, square, 0) < lax.broadcasted_iota(jnp.int32, square, 1)
    if group_blocks > 1:
        earlier = earlier & (block_of(0, square) == block_of(1, square))
    earlier = earlier.astype(F32).astype(BF16)

    loads[1].wait()
    loads[2].wait()
    pl.semaphore_wait(barrier, devices - 1)
    own_group = lax.div(sec, group_blocks)

    def one_group(step, carry):
        which = lax.rem(own_group + 1 + step, groups)
        spectra[...] = jnp.dot(filtered[...], table[which], preferred_element_type=F32)
        total = [[[None] * frames for _ in range(2)] for _ in range(2)]
        channels = pl.ds(pl.multiple_of(which * group, group), group)
        for entry in range(inputs):
            weight = weights[entry, :, channels].astype(F32)
            weight_r, weight_i = weight[:beams], weight[beams:]
            mine = total[entry % 2]
            for frame in range(frames):
                row = frame * inputs + entry
                real = spectra[row : row + 1, :group]
                imag = spectra[row : row + 1, group:]
                sum_r = weight_r * real - weight_i * imag
                sum_i = weight_r * imag + weight_i * real
                mine[0][frame] = sum_r if mine[0][frame] is None else mine[0][frame] + sum_r
                mine[1][frame] = sum_i if mine[1][frame] is None else mine[1][frame] + sum_i
        shares = jnp.concatenate(
            [total[p][part][f] * inside for p in range(2) for part in range(2) for f in range(frames)],
            axis=0,
        ).astype(BF16)
        owner = owner_ref[which]
        owned = lax.broadcasted_iota(jnp.int32, (stations, group), 0) == owner
        ahead = jnp.dot(owned.astype(F32).astype(BF16), earlier, preferred_element_type=F32)
        rank = jnp.sum(jnp.where(owned, ahead, 0.0), axis=0, keepdims=True).astype(jnp.int32)
        slot = (block_of(1, (1, group)) * stations + owner) * rows + rank
        order = lax.broadcasted_iota(jnp.int32, (group_targets * rows, group), 0) == slot
        ordered = lax.dot_general(
            order.astype(F32).astype(BF16), shares, (((1,), (1,)), ((), ())),
            preferred_element_type=F32,
        )
        base = which * group_targets
        outgoing[pl.ds(base, group_targets)] = ordered.astype(BF16).reshape(group_targets, rows, LANES)

        def send(turn, inner):
            part = lax.div(turn, stations)
            to_st = lax.rem(st + turn, stations)
            target = base + part * stations + to_st

            @pl.when(target != me)
            def _():
                pltpu.make_async_remote_copy(
                    src_ref=outgoing.at[target], dst_ref=arrived.at[me],
                    send_sem=send_sem, recv_sem=recv_sem,
                    device_id=(to_st, which * group_blocks + part), device_id_type=MESH,
                ).start()

            return inner

        lax.fori_loop(0, group_targets, send, 0)
        return carry

    lax.fori_loop(0, groups, one_group, 0)

    arrived[me] = outgoing[me]
    others = pl.ds(0, devices - 1)
    pltpu.make_async_copy(arrived.at[others], arrived.at[others], recv_sem).wait()
    summed = arrived[0:stations].astype(F32)
    for other in range(1, sections):
        summed = summed + arrived[other * stations : (other + 1) * stations].astype(F32)
    out_ref[...] = summed.astype(BF16).reshape(stations * rows, LANES)
    pltpu.make_async_copy(outgoing.at[others], outgoing.at[others], send_sem).wait()


def correlate_kernel(dims, beams_ref, place_ref, out_hbm, left, right, mask, result, sem):
    beams, frames, per_owner, signals = dims
    half = frames * beams
    spread = jnp.dot(place_ref[...], beams_ref[...], preferred_element_type=F32)
    shape = spread.shape
    lane = lax.broadcasted_iota(jnp.int32, shape, 1)
    odd = (lax.broadcasted_iota(jnp.int32, shape, 0) & 1) == 1
    both = jnp.where(odd, pltpu.roll(spread, 2 * half, 1), spread)
    turned = jnp.where(lane < half, -pltpu.roll(both, LANES - half, 1), pltpu.roll(both, half, 1))
    left[...] = both.astype(BF16).reshape(per_owner, signals, LANES)
    right[:, :signals] = left[...]
    right[:, signals:] = turned.astype(BF16).reshape(per_owner, signals, LANES)
    full = (beams, frames, signals, LANES)
    column = lax.broadcasted_iota(jnp.int32, full, 1) * beams + lax.broadcasted_iota(jnp.int32, full, 0)
    lane = lax.broadcasted_iota(jnp.int32, full, 3)
    hit = (lane == column) | (lane == column + half)
    mask[...] = hit.astype(F32).astype(BF16).reshape(half, signals, LANES)

    def channel(at, carry):
        masked = (left[at][None] * mask[...]).reshape(half * signals, LANES)
        product = lax.dot_general(
            masked, right[at], (((1,), (1,)), ((), ())), preferred_element_type=F32
        )
        result[at] = product.astype(BF16).reshape(beams, frames, signals, 2 * signals)
        pltpu.make_async_copy(result.at[at], out_hbm.at[0, 0, at], sem).start()
        return carry

    lax.fori_loop(0, per_owner, channel, 0)
    pltpu.make_async_copy(result, out_hbm.at[0, 0], sem).wait()


def local(voltages, taper, beam_weight_table, starts, owner_map):
    inputs = voltages.shape[1]
    taps, length = taper.shape
    frames = voltages.shape[2] // length - taps + 1
    channels = length // 2
    beams = beam_weight_table.shape[1]
    sections = lax.axis_size("section")
    stations = lax.axis_size("station")
    block = channels // sections
    per_owner = block // stations
    group = max(LANES, block)
    groups = channels // group
    rows = -(-per_owner // 16) * 16
    devices = sections * stations
    signals = 2 * stations
    values = 4 * frames * beams
    dims = (sections, stations, inputs, frames, taps, length, beams, group, block, per_owner, rows)

    weights = jnp.transpose(beam_weight_table[0], (1, 2, 0, 3)).reshape(inputs, 2 * beams, channels)
    table = jnp.asarray(dft_table(length, group))
    owners = owner_map.reshape(groups, 1, group)
    vmem = pl.BlockSpec(memory_space=pltpu.VMEM)
    hbm = pl.BlockSpec(memory_space=pl.ANY)
    mine = pl.pallas_call(
        functools.partial(beam_kernel, dims),
        out_shape=jax.ShapeDtypeStruct((stations * rows, values), BF16),
        in_specs=[pl.BlockSpec(memory_space=pltpu.SMEM), vmem, vmem, hbm, hbm, hbm],
        out_specs=vmem,
        scratch_shapes=[
            pltpu.VMEM(voltages.shape[1:], BF16),
            pltpu.VMEM(weights.shape, BF16),
            pltpu.VMEM(table.shape, BF16),
            pltpu.VMEM((frames * inputs, length), BF16),
            pltpu.VMEM((frames * inputs, 2 * group), F32),
            pltpu.VMEM((devices, rows, values), BF16),
            pltpu.VMEM((devices, rows, values), BF16),
            pltpu.SemaphoreType.DMA((3,)),
            pltpu.SemaphoreType.DMA,
            pltpu.SemaphoreType.DMA,
        ],
        compiler_params=pltpu.CompilerParams(
            collective_id=0, has_side_effects=True, vmem_limit_bytes=40 * 1024 * 1024
        ),
    )(starts, owners, taper, voltages, weights, table)

    place = np.zeros((per_owner, stations, 2, stations, rows), np.float32)
    for at in range(per_owner):
        for station in range(stations):
            place[at, station, :, station, at] = 1.0
    place = jnp.asarray(place.reshape(per_owner * signals, stations * rows).astype(jnp.bfloat16))
    return pl.pallas_call(
        functools.partial(correlate_kernel, (beams, frames, per_owner, signals)),
        out_shape=jax.ShapeDtypeStruct(
            (1, 1, per_owner, beams, frames, signals, 2 * signals), BF16
        ),
        in_specs=[vmem, vmem],
        out_specs=hbm,
        scratch_shapes=[
            pltpu.VMEM((per_owner, signals, LANES), BF16),
            pltpu.VMEM((per_owner, 2 * signals, LANES), BF16),
            pltpu.VMEM((frames * beams, signals, LANES), BF16),
            pltpu.VMEM((per_owner, beams, frames, signals, 2 * signals), BF16),
            pltpu.SemaphoreType.DMA,
        ],
        compiler_params=pltpu.CompilerParams(vmem_limit_bytes=40 * 1024 * 1024),
    )(mine, place)


def solution(mesh):
    placed = (
        P("station", "section", None),
        P(),
        P("station", None, "section", None, None),
        P(),
        P(),
    )
    return jax.shard_map(
        local,
        mesh=mesh,
        in_specs=placed,
        out_specs=P("section", "station", None, None, None, None, None),
        check_vma=False,
    )
```

```python
import functools
import math

import jax
import jax.numpy as jnp
import numpy as np
from jax import lax
from jax.experimental import pallas as pl
from jax.experimental.pallas import tpu as pltpu
from jax.sharding import PartitionSpec as P

MESH = pl.DeviceIdType.MESH
LANES = 128
VMEM_LIMIT = 60 * 1024 * 1024
F32 = jnp.float32
BF16 = jnp.bfloat16


def dft_table(length, group):
    half = length // 2
    index_n = np.arange(length, dtype=np.int64)[:, None]
    index_k = np.arange(half, dtype=np.int64)[None, :]
    phase = (index_n * index_k % length).astype(np.float32) * np.float32(2.0 * math.pi / length)
    factor = np.float32(1.0 / math.sqrt(length))
    real = (np.cos(phase) * factor).reshape(length, half // group, group)
    imag = (-np.sin(phase) * factor).reshape(length, half // group, group)
    return np.concatenate([real, imag], axis=2).transpose(1, 0, 2).astype(jnp.bfloat16)


def beam_kernel(
    dims, starts_hbm, owner_hbm, taper_hbm, volts_hbm, weights_hbm, table_hbm, out_ref,
    starts_ref, owner_ref, taper_ref, volts, weights, table, filtered, spectra_a, spectra_b, orders,
    outgoing, arrived, load_sems, send_sem, recv_sem,
):
    sections, stations, inputs, frames, taps, length, beams, group, block, per_owner, rows = dims
    st = lax.axis_index("station")
    sec = lax.axis_index("section")
    devices = sections * stations
    me = sec * stations + st
    groups = table.shape[0]
    group_blocks = group // block
    group_targets = group_blocks * stations

    own_group = lax.div(sec, group_blocks)
    turns = [lax.rem(own_group + 1 + step, groups) for step in range(groups)]
    pairs = [(volts_hbm.at[0], volts), (taper_hbm, taper_ref), (owner_hbm, owner_ref), (starts_hbm, starts_ref)]
    pairs += [(table_hbm.at[turn], table.at[turn]) for turn in turns[:1]]
    pairs += [(weights_hbm, weights)]
    pairs += [(table_hbm.at[turn], table.at[turn]) for turn in turns[1:]]
    loads = [
        pltpu.make_async_copy(here, there, load_sems.at[at]) for at, (here, there) in enumerate(pairs)
    ]
    for load in loads:
        load.start()

    barrier = pltpu.get_barrier_semaphore()

    def greet(step, carry):
        other = lax.rem(me + step, devices)
        pl.semaphore_signal(
            barrier, inc=1, device_id=(lax.rem(other, stations), lax.div(other, stations)),
            device_id_type=MESH,
        )
        return carry

    lax.fori_loop(1, devices, greet, 0)

    def block_of(axis, shape):
        at = lax.broadcasted_iota(jnp.int32, shape, axis)
        total = jnp.zeros(shape, jnp.int32)
        for edge in range(1, group_blocks):
            total = total + (at >= edge * block).astype(jnp.int32)
        return total

    square = (group, group)
    earlier = lax.broadcasted_iota(jnp.int32, square, 0) < lax.broadcasted_iota(jnp.int32, square, 1)
    if group_blocks > 1:
        earlier = earlier & (block_of(0, square) == block_of(1, square))
    earlier = earlier.astype(F32).astype(BF16)

    loads[2].wait()

    def make_order(which, carry):
        owner = owner_ref[which]
        owned = lax.broadcasted_iota(jnp.int32, (stations, group), 0) == owner
        ahead = jnp.dot(owned.astype(F32).astype(BF16), earlier, preferred_element_type=F32)
        rank = jnp.sum(jnp.where(owned, ahead, 0.0), axis=0, keepdims=True).astype(jnp.int32)
        slot = (block_of(1, (1, group)) * stations + owner) * rows + rank
        order = lax.broadcasted_iota(jnp.int32, (group_targets * rows, group), 0) == slot
        orders[which] = order.astype(F32).astype(BF16)
        return carry

    lax.fori_loop(0, groups, make_order, 0)

    loads[0].wait()
    loads[1].wait()

    def filter_chunk(chunk, carry):
        at = pl.multiple_of(chunk * LANES, LANES)
        sums = [None] * frames
        for segment in range(frames + taps - 1):
            lanes = pl.ds(pl.multiple_of(segment * length + at, LANES), LANES)
            part = volts[:, lanes].astype(F32)
            for frame in range(frames):
                tap = segment - frame
                if 0 <= tap < taps:
                    term = taper_ref[tap : tap + 1, pl.ds(at, LANES)] * part
                    sums[frame] = term if sums[frame] is None else sums[frame] + term
        for frame in range(frames):
            filtered[frame * inputs : (frame + 1) * inputs, pl.ds(at, LANES)] = sums[frame].astype(BF16)
        return carry

    lax.fori_loop(0, length // LANES, filter_chunk, 0)

    loads[3].wait()
    beam_row = lax.broadcasted_iota(jnp.int32, (beams, group), 0)
    first = jnp.zeros((beams, group), jnp.int32)
    for beam in range(beams):
        first = jnp.where(beam_row == beam, starts_ref[beam], first)
    offset = sec - first
    offset = jnp.where(offset < 0, offset + sections, offset)
    inside = (offset < max(1, sections // 2)).astype(F32)

    def transform(step):
        target = (spectra_a, spectra_b)[step % 2]
        target[...] = jnp.dot(filtered[...], table[turns[step]], preferred_element_type=F32)

    loads[4].wait()
    transform(0)
    loads[5].wait()
    pl.semaphore_wait(barrier, devices - 1)

    for step in range(groups):
        which = turns[step]
        spectra = (spectra_a, spectra_b)[step % 2]
        if step + 1 < groups:
            loads[6 + step].wait()
            transform(step + 1)
        total = [[[None] * frames for _ in range(2)] for _ in range(2)]
        channels = pl.ds(pl.multiple_of(which * group, group), group)
        for entry in range(inputs):
            weight = weights[entry, :, channels].astype(F32)
            weight_r, weight_i = weight[:beams], weight[beams:]
            mine = total[entry % 2]
            for frame in range(frames):
                row = frame * inputs + entry
                real = spectra[row : row + 1, :group]
                imag = spectra[row : row + 1, group:]
                sum_r = weight_r * real - weight_i * imag
                sum_i = weight_r * imag + weight_i * real
                mine[0][frame] = sum_r if mine[0][frame] is None else mine[0][frame] + sum_r
                mine[1][frame] = sum_i if mine[1][frame] is None else mine[1][frame] + sum_i
        shares = jnp.concatenate(
            [total[p][part][f] * inside for p in range(2) for part in range(2) for f in range(frames)],
            axis=0,
        ).astype(BF16)
        ordered = lax.dot_general(
            orders[which], shares, (((1,), (1,)), ((), ())), preferred_element_type=F32
        )
        base = which * group_targets
        outgoing[pl.ds(base, group_targets)] = ordered.astype(BF16).reshape(group_targets, rows, LANES)

        def send(turn, carry):
            part = lax.div(turn, stations)
            to_st = lax.rem(st + turn, stations)
            target = base + part * stations + to_st

            @pl.when(target != me)
            def _():
                pltpu.make_async_remote_copy(
                    src_ref=outgoing.at[target], dst_ref=arrived.at[me],
                    send_sem=send_sem, recv_sem=recv_sem,
                    device_id=(to_st, which * group_blocks + part), device_id_type=MESH,
                ).start()

            return carry

        lax.fori_loop(0, group_targets, send, 0)

    arrived[me] = outgoing[me]
    others = pl.ds(0, devices - 1)
    pltpu.make_async_copy(arrived.at[others], arrived.at[others], recv_sem).wait()
    summed = arrived[0:stations].astype(F32)
    for other in range(1, sections):
        summed = summed + arrived[other * stations : (other + 1) * stations].astype(F32)
    out_ref[...] = summed.astype(BF16).reshape(stations * rows, LANES)
    pltpu.make_async_copy(outgoing.at[others], outgoing.at[others], send_sem).wait()


def correlate_kernel(dims, beams_ref, place_ref, out_hbm, left, right, mask, result, sem):
    beams, frames, per_owner, signals = dims
    half = frames * beams
    spread = jnp.dot(place_ref[...], beams_ref[...], preferred_element_type=F32)
    shape = spread.shape
    lane = lax.broadcasted_iota(jnp.int32, shape, 1)
    odd = (lax.broadcasted_iota(jnp.int32, shape, 0) & 1) == 1
    both = jnp.where(odd, pltpu.roll(spread, 2 * half, 1), spread)
    turned = jnp.where(lane < half, -pltpu.roll(both, LANES - half, 1), pltpu.roll(both, half, 1))
    left[...] = both.astype(BF16).reshape(per_owner, signals, LANES)
    right[:, :signals] = left[...]
    right[:, signals:] = turned.astype(BF16).reshape(per_owner, signals, LANES)
    full = (beams, frames, signals, LANES)
    column = lax.broadcasted_iota(jnp.int32, full, 1) * beams + lax.broadcasted_iota(jnp.int32, full, 0)
    lane = lax.broadcasted_iota(jnp.int32, full, 3)
    hit = (lane == column) | (lane == column + half)
    mask[...] = hit.astype(F32).astype(BF16).reshape(half, signals, LANES)

    batch = math.gcd(4, per_owner)

    def channels(step, carry):
        first = step * batch
        products = []
        for at in range(batch):
            masked = (left[first + at][None] * mask[...]).reshape(half * signals, LANES)
            products.append(
                lax.dot_general(
                    masked, right[first + at], (((1,), (1,)), ((), ())), preferred_element_type=F32
                )
            )
        for at in range(batch):
            result[first + at] = products[at].astype(BF16).reshape(beams, frames, signals, 2 * signals)
        several = pl.ds(first, batch)
        pltpu.make_async_copy(result.at[several], out_hbm.at[0, 0, several], sem).start()
        return carry

    lax.fori_loop(0, per_owner // batch, channels, 0)
    pltpu.make_async_copy(result, out_hbm.at[0, 0], sem).wait()


def local(voltages, taper, beam_weight_table, starts, owner_map):
    inputs = voltages.shape[1]
    taps, length = taper.shape
    frames = voltages.shape[2] // length - taps + 1
    channels = length // 2
    beams = beam_weight_table.shape[1]
    sections = lax.axis_size("section")
    stations = lax.axis_size("station")
    block = channels // sections
    per_owner = block // stations
    group = max(LANES, block)
    groups = channels // group
    rows = -(-per_owner // 16) * 16
    devices = sections * stations
    signals = 2 * stations
    values = 4 * frames * beams
    dims = (sections, stations, inputs, frames, taps, length, beams, group, block, per_owner, rows)

    weights = jnp.transpose(beam_weight_table[0], (1, 2, 0, 3)).reshape(inputs, 2 * beams, channels)
    table = jnp.asarray(dft_table(length, group))
    owners = owner_map.reshape(groups, 1, group)
    vmem = pl.BlockSpec(memory_space=pltpu.VMEM)
    hbm = pl.BlockSpec(memory_space=pl.ANY)
    mine = pl.pallas_call(
        functools.partial(beam_kernel, dims),
        out_shape=jax.ShapeDtypeStruct((stations * rows, values), BF16),
        in_specs=[hbm] * 6,
        out_specs=vmem,
        scratch_shapes=[
            pltpu.SMEM(starts.shape, jnp.int32),
            pltpu.VMEM(owners.shape, jnp.int32),
            pltpu.VMEM(taper.shape, F32),
            pltpu.VMEM(voltages.shape[1:], BF16),
            pltpu.VMEM(weights.shape, BF16),
            pltpu.VMEM(table.shape, BF16),
            pltpu.VMEM((frames * inputs, length), BF16),
            pltpu.VMEM((frames * inputs, 2 * group), F32),
            pltpu.VMEM((frames * inputs, 2 * group), F32),
            pltpu.VMEM((groups, group // per_owner * rows, group), BF16),
            pltpu.VMEM((devices, rows, values), BF16),
            pltpu.VMEM((devices, rows, values), BF16),
            pltpu.SemaphoreType.DMA((5 + groups,)),
            pltpu.SemaphoreType.DMA,
            pltpu.SemaphoreType.DMA,
        ],
        compiler_params=pltpu.CompilerParams(
            collective_id=0, has_side_effects=True, vmem_limit_bytes=VMEM_LIMIT
        ),
    )(starts, owners, taper, voltages, weights, table)

    place = np.zeros((per_owner, stations, 2, stations, rows), np.float32)
    for at in range(per_owner):
        for station in range(stations):
            place[at, station, :, station, at] = 1.0
    place = jnp.asarray(place.reshape(per_owner * signals, stations * rows).astype(jnp.bfloat16))
    return pl.pallas_call(
        functools.partial(correlate_kernel, (beams, frames, per_owner, signals)),
        out_shape=jax.ShapeDtypeStruct(
            (1, 1, per_owner, beams, frames, signals, 2 * signals), BF16
        ),
        in_specs=[vmem, vmem],
        out_specs=hbm,
        scratch_shapes=[
            pltpu.VMEM((per_owner, signals, LANES), BF16),
            pltpu.VMEM((per_owner, 2 * signals, LANES), BF16),
            pltpu.VMEM((frames * beams, signals, LANES), BF16),
            pltpu.VMEM((per_owner, beams, frames, signals, 2 * signals), BF16),
            pltpu.SemaphoreType.DMA,
        ],
        compiler_params=pltpu.CompilerParams(vmem_limit_bytes=32 * 1024 * 1024),
    )(mine, place)


def solution(mesh):
    placed = (
        P("station", "section", None),
        P(),
        P("station", None, "section", None, None),
        P(),
        P(),
    )
    return jax.shard_map(
        local,
        mesh=mesh,
        in_specs=placed,
        out_specs=P("section", "station", None, None, None, None, None),
        check_vma=False,
    )
```

```python
import functools
import math

import jax
import jax.numpy as jnp
import numpy as np
from jax import lax
from jax.experimental import pallas as pl
from jax.experimental.pallas import tpu as pltpu
from jax.sharding import PartitionSpec as P

MESH = pl.DeviceIdType.MESH
LANES = 128
VMEM_LIMIT = 60 * 1024 * 1024
F32 = jnp.float32
BF16 = jnp.bfloat16


def dft_table(length, group):
    half = length // 2
    index_n = np.arange(length, dtype=np.int64)[:, None]
    index_k = np.arange(half, dtype=np.int64)[None, :]
    phase = (index_n * index_k % length).astype(np.float32) * np.float32(2.0 * math.pi / length)
    factor = np.float32(1.0 / math.sqrt(length))
    real = (np.cos(phase) * factor).reshape(length, half // group, group)
    imag = (-np.sin(phase) * factor).reshape(length, half // group, group)
    return np.concatenate([real, imag], axis=2).transpose(1, 0, 2).astype(jnp.bfloat16)


def beam_kernel(
    dims, starts_hbm, owner_hbm, taper_hbm, volts_hbm, weights_hbm, table_hbm, out_ref,
    starts_ref, owner_ref, taper_ref, volts, weights, wide, table, filtered, spectra_a, spectra_b, orders,
    outgoing, arrived, load_sems, send_sem, recv_sem,
):
    sections, stations, inputs, frames, taps, length, beams, group, block, per_owner, rows = dims
    st = lax.axis_index("station")
    sec = lax.axis_index("section")
    devices = sections * stations
    me = sec * stations + st
    groups = table.shape[0]
    group_blocks = group // block
    group_targets = group_blocks * stations

    own_group = lax.div(sec, group_blocks)
    turns = [lax.rem(own_group + 1 + step, groups) for step in range(groups)]
    pairs = [
        (owner_hbm, owner_ref), (weights_hbm.at[0], weights), (volts_hbm.at[0], volts),
        (taper_hbm, taper_ref), (starts_hbm, starts_ref),
    ]
    pairs += [(table_hbm.at[turn], table.at[turn]) for turn in turns]
    loads = [
        pltpu.make_async_copy(here, there, load_sems.at[at]) for at, (here, there) in enumerate(pairs)
    ]
    for load in loads:
        load.start()

    barrier = pltpu.get_barrier_semaphore()

    def greet(step, carry):
        other = lax.rem(me + step, devices)
        pl.semaphore_signal(
            barrier, inc=1, device_id=(lax.rem(other, stations), lax.div(other, stations)),
            device_id_type=MESH,
        )
        return carry

    lax.fori_loop(1, devices, greet, 0)

    def block_of(axis, shape):
        at = lax.broadcasted_iota(jnp.int32, shape, axis)
        total = jnp.zeros(shape, jnp.int32)
        for edge in range(1, group_blocks):
            total = total + (at >= edge * block).astype(jnp.int32)
        return total

    square = (group, group)
    earlier = lax.broadcasted_iota(jnp.int32, square, 0) < lax.broadcasted_iota(jnp.int32, square, 1)
    if group_blocks > 1:
        earlier = earlier & (block_of(0, square) == block_of(1, square))
    earlier = earlier.astype(F32).astype(BF16)

    loads[0].wait()

    def make_order(which, carry):
        owner = owner_ref[which]
        owned = lax.broadcasted_iota(jnp.int32, (stations, group), 0) == owner
        ahead = jnp.dot(owned.astype(F32).astype(BF16), earlier, preferred_element_type=F32)
        rank = jnp.sum(jnp.where(owned, ahead, 0.0), axis=0, keepdims=True).astype(jnp.int32)
        slot = (block_of(1, (1, group)) * stations + owner) * rows + rank
        order = lax.broadcasted_iota(jnp.int32, (group_targets * rows, group), 0) == slot
        orders[which] = order.astype(F32).astype(BF16)
        return carry

    lax.fori_loop(0, groups, make_order, 0)

    loads[1].wait()
    few = 4

    def widen(step, carry):
        beam, at = lax.div(step, inputs // few), lax.rem(step, inputs // few)
        part = weights[beam, pl.ds(at * few, few)].astype(F32).reshape(2 * few, groups * group)
        for which in range(groups):
            wide[which, pl.ds(step * 2 * few, 2 * few), :] = part[:, which * group : (which + 1) * group]
        return carry

    lax.fori_loop(0, beams * inputs // few, widen, 0, unroll=4)

    loads[2].wait()
    loads[3].wait()

    def filter_chunk(chunk, carry):
        at = pl.multiple_of(chunk * LANES, LANES)
        sums = [None] * frames
        for segment in range(frames + taps - 1):
            lanes = pl.ds(pl.multiple_of(segment * length + at, LANES), LANES)
            part = volts[:, lanes].astype(F32)
            for frame in range(frames):
                tap = segment - frame
                if 0 <= tap < taps:
                    term = taper_ref[tap : tap + 1, pl.ds(at, LANES)] * part
                    sums[frame] = term if sums[frame] is None else sums[frame] + term
        for frame in range(frames):
            filtered[frame * inputs : (frame + 1) * inputs, pl.ds(at, LANES)] = sums[frame].astype(BF16)
        return carry

    lax.fori_loop(0, length // LANES, filter_chunk, 0)

    loads[4].wait()
    beam_row = lax.broadcasted_iota(jnp.int32, (beams, group), 0)
    first = jnp.zeros((beams, group), jnp.int32)
    for beam in range(beams):
        first = jnp.where(beam_row == beam, starts_ref[beam], first)
    offset = sec - first
    offset = jnp.where(offset < 0, offset + sections, offset)
    inside = (offset < max(1, sections // 2)).astype(F32)

    def transform(step):
        target = (spectra_a, spectra_b)[step % 2]
        target[...] = jnp.dot(filtered[...], table[turns[step]], preferred_element_type=F32)

    loads[5].wait()
    transform(0)
    pl.semaphore_wait(barrier, devices - 1)

    for step in range(groups):
        which = turns[step]
        spectra = (spectra_a, spectra_b)[step % 2]
        if step + 1 < groups:
            loads[6 + step].wait()
            transform(step + 1)
        total = [[[None] * frames for _ in range(2)] for _ in range(2)]
        for entry in range(inputs):
            weight_r = wide[which, pl.ds(2 * entry, beams, stride=2 * inputs), :]
            weight_i = wide[which, pl.ds(2 * entry + 1, beams, stride=2 * inputs), :]
            mine = total[entry % 2]
            for frame in range(frames):
                row = frame * inputs + entry
                real = spectra[row : row + 1, :group]
                imag = spectra[row : row + 1, group:]
                sum_r = weight_r * real - weight_i * imag
                sum_i = weight_r * imag + weight_i * real
                mine[0][frame] = sum_r if mine[0][frame] is None else mine[0][frame] + sum_r
                mine[1][frame] = sum_i if mine[1][frame] is None else mine[1][frame] + sum_i
        shares = jnp.concatenate(
            [total[p][part][f] * inside for p in range(2) for part in range(2) for f in range(frames)],
            axis=0,
        ).astype(BF16)
        ordered = lax.dot_general(
            orders[which], shares, (((1,), (1,)), ((), ())), preferred_element_type=F32
        )
        base = which * group_targets
        outgoing[pl.ds(base, group_targets)] = ordered.astype(BF16).reshape(group_targets, rows, LANES)

        def send(turn, carry):
            part = lax.div(turn, stations)
            to_st = lax.rem(st + turn, stations)
            target = base + part * stations + to_st

            @pl.when(target != me)
            def _():
                pltpu.make_async_remote_copy(
                    src_ref=outgoing.at[target], dst_ref=arrived.at[me],
                    send_sem=send_sem, recv_sem=recv_sem,
                    device_id=(to_st, which * group_blocks + part), device_id_type=MESH,
                ).start()

            return carry

        lax.fori_loop(0, group_targets, send, 0)

    arrived[me] = outgoing[me]
    others = pl.ds(0, devices - 1)
    pltpu.make_async_copy(arrived.at[others], arrived.at[others], recv_sem).wait()
    summed = arrived[0:stations].astype(F32)
    for other in range(1, sections):
        summed = summed + arrived[other * stations : (other + 1) * stations].astype(F32)
    out_ref[...] = summed.astype(BF16).reshape(stations * rows, LANES)
    pltpu.make_async_copy(outgoing.at[others], outgoing.at[others], send_sem).wait()


def correlate_kernel(
    dims, beams_hbm, place_hbm, out_hbm, beams_ref, place_ref, left, right, mask, result, sems, sem
):
    beams, frames, per_owner, signals = dims
    half = frames * beams
    loads = [
        pltpu.make_async_copy(beams_hbm, beams_ref, sems.at[0]),
        pltpu.make_async_copy(place_hbm, place_ref, sems.at[1]),
    ]
    for load in loads:
        load.start()
    full = (beams, frames, signals, LANES)
    column = lax.broadcasted_iota(jnp.int32, full, 1) * beams + lax.broadcasted_iota(jnp.int32, full, 0)
    lane = lax.broadcasted_iota(jnp.int32, full, 3)
    hit = (lane == column) | (lane == column + half)
    mask[...] = hit.astype(F32).astype(BF16).reshape(half, signals, LANES)
    for load in loads:
        load.wait()
    spread = jnp.dot(place_ref[...], beams_ref[...], preferred_element_type=F32)
    shape = spread.shape
    lane = lax.broadcasted_iota(jnp.int32, shape, 1)
    odd = (lax.broadcasted_iota(jnp.int32, shape, 0) & 1) == 1
    both = jnp.where(odd, pltpu.roll(spread, 2 * half, 1), spread)
    turned = jnp.where(lane < half, -pltpu.roll(both, LANES - half, 1), pltpu.roll(both, half, 1))
    left[...] = both.astype(BF16).reshape(per_owner, signals, LANES)
    right[:, :signals] = left[...]
    right[:, signals:] = turned.astype(BF16).reshape(per_owner, signals, LANES)

    batch = math.gcd(4, per_owner)

    def channels(step, carry):
        first = step * batch
        products = []
        for at in range(batch):
            masked = (left[first + at][None] * mask[...]).reshape(half * signals, LANES)
            products.append(
                lax.dot_general(
                    masked, right[first + at], (((1,), (1,)), ((), ())), preferred_element_type=F32
                )
            )
        for at in range(batch):
            result[first + at] = products[at].astype(BF16).reshape(beams, frames, signals, 2 * signals)
        several = pl.ds(first, batch)
        pltpu.make_async_copy(result.at[several], out_hbm.at[0, 0, several], sem).start()
        return carry

    lax.fori_loop(0, per_owner // batch, channels, 0)
    pltpu.make_async_copy(result, out_hbm.at[0, 0], sem).wait()


def local(voltages, taper, beam_weight_table, starts, owner_map):
    inputs = voltages.shape[1]
    taps, length = taper.shape
    frames = voltages.shape[2] // length - taps + 1
    channels = length // 2
    beams = beam_weight_table.shape[1]
    sections = lax.axis_size("section")
    stations = lax.axis_size("station")
    block = channels // sections
    per_owner = block // stations
    group = max(LANES, block)
    groups = channels // group
    rows = -(-per_owner // 16) * 16
    devices = sections * stations
    signals = 2 * stations
    values = 4 * frames * beams
    dims = (sections, stations, inputs, frames, taps, length, beams, group, block, per_owner, rows)

    table = jnp.asarray(dft_table(length, group))
    owners = owner_map.reshape(groups, 1, group)
    vmem = pl.BlockSpec(memory_space=pltpu.VMEM)
    hbm = pl.BlockSpec(memory_space=pl.ANY)
    mine = pl.pallas_call(
        functools.partial(beam_kernel, dims),
        out_shape=jax.ShapeDtypeStruct((stations * rows, values), BF16),
        in_specs=[hbm] * 6,
        out_specs=vmem,
        scratch_shapes=[
            pltpu.SMEM(starts.shape, jnp.int32),
            pltpu.VMEM(owners.shape, jnp.int32),
            pltpu.VMEM(taper.shape, F32),
            pltpu.VMEM(voltages.shape[1:], BF16),
            pltpu.VMEM(beam_weight_table.shape[1:], BF16),
            pltpu.VMEM((groups, 2 * beams * inputs, group), F32),
            pltpu.VMEM(table.shape, BF16),
            pltpu.VMEM((frames * inputs, length), BF16),
            pltpu.VMEM((frames * inputs, 2 * group), F32),
            pltpu.VMEM((frames * inputs, 2 * group), F32),
            pltpu.VMEM((groups, group // per_owner * rows, group), BF16),
            pltpu.VMEM((devices, rows, values), BF16),
            pltpu.VMEM((devices, rows, values), BF16),
            pltpu.SemaphoreType.DMA((5 + groups,)),
            pltpu.SemaphoreType.DMA,
            pltpu.SemaphoreType.DMA,
        ],
        compiler_params=pltpu.CompilerParams(
            collective_id=0, has_side_effects=True, vmem_limit_bytes=VMEM_LIMIT
        ),
    )(starts, owners, taper, voltages, beam_weight_table, table)

    place = np.zeros((per_owner, stations, 2, stations, rows), np.float32)
    for at in range(per_owner):
        for station in range(stations):
            place[at, station, :, station, at] = 1.0
    place = jnp.asarray(place.reshape(per_owner * signals, stations * rows).astype(jnp.bfloat16))
    return pl.pallas_call(
        functools.partial(correlate_kernel, (beams, frames, per_owner, signals)),
        out_shape=jax.ShapeDtypeStruct(
            (1, 1, per_owner, beams, frames, signals, 2 * signals), BF16
        ),
        in_specs=[hbm, hbm],
        out_specs=hbm,
        scratch_shapes=[
            pltpu.VMEM(mine.shape, BF16),
            pltpu.VMEM(place.shape, BF16),
            pltpu.VMEM((per_owner, signals, LANES), BF16),
            pltpu.VMEM((per_owner, 2 * signals, LANES), BF16),
            pltpu.VMEM((frames * beams, signals, LANES), BF16),
            pltpu.VMEM((per_owner, beams, frames, signals, 2 * signals), BF16),
            pltpu.SemaphoreType.DMA((2,)),
            pltpu.SemaphoreType.DMA,
        ],
        compiler_params=pltpu.CompilerParams(vmem_limit_bytes=VMEM_LIMIT),
    )(mine, place)


def solution(mesh):
    placed = (
        P("station", "section", None),
        P(),
        P("station", None, "section", None, None),
        P(),
        P(),
    )
    return jax.shard_map(
        local,
        mesh=mesh,
        in_specs=placed,
        out_specs=P("section", "station", None, None, None, None, None),
        check_vma=False,
    )
```

```python
import functools
import math

import jax
import jax.numpy as jnp
import numpy as np
from jax import lax
from jax.experimental import pallas as pl
from jax.experimental.pallas import tpu as pltpu
from jax.sharding import PartitionSpec as P

MESH = pl.DeviceIdType.MESH
LANES = 128
VMEM_LIMIT = 60 * 1024 * 1024
F32 = jnp.float32
BF16 = jnp.bfloat16


def dft_table(length, group):
    half = length // 2
    index_n = np.arange(length, dtype=np.int64)[:, None]
    index_k = np.arange(half, dtype=np.int64)[None, :]
    phase = (index_n * index_k % length).astype(np.float32) * np.float32(2.0 * math.pi / length)
    factor = np.float32(1.0 / math.sqrt(length))
    real = (np.cos(phase) * factor).reshape(length, half // group, group)
    imag = (-np.sin(phase) * factor).reshape(length, half // group, group)
    return np.concatenate([real, imag], axis=2).transpose(1, 0, 2).astype(jnp.bfloat16)


def beam_kernel(
    dims, starts_hbm, owner_hbm, taper_hbm, volts_hbm, weights_hbm, table_hbm, out_ref,
    starts_ref, owner_ref, taper_ref, volts, weights, wide, table, filtered, spectra_a, spectra_b, orders,
    outgoing, arrived, load_sems, send_sem, recv_sem,
):
    sections, stations, inputs, frames, taps, length, beams, group, block, per_owner, rows = dims
    st = lax.axis_index("station")
    sec = lax.axis_index("section")
    devices = sections * stations
    me = sec * stations + st
    groups = table.shape[0]
    group_blocks = group // block
    group_targets = group_blocks * stations

    own_group = lax.div(sec, group_blocks)
    turns = [lax.rem(own_group + 1 + step, groups) for step in range(groups)]
    pairs = [
        (owner_hbm, owner_ref), (weights_hbm.at[0], weights), (volts_hbm.at[0], volts),
        (taper_hbm, taper_ref), (starts_hbm, starts_ref),
    ]
    pairs += [(table_hbm.at[turn], table.at[turn]) for turn in turns]
    loads = [
        pltpu.make_async_copy(here, there, load_sems.at[at]) for at, (here, there) in enumerate(pairs)
    ]
    for load in loads:
        load.start()

    barrier = pltpu.get_barrier_semaphore()

    def greet(step, carry):
        other = lax.rem(me + step, devices)
        pl.semaphore_signal(
            barrier, inc=1, device_id=(lax.rem(other, stations), lax.div(other, stations)),
            device_id_type=MESH,
        )
        return carry

    lax.fori_loop(1, devices, greet, 0)

    def block_of(axis, shape):
        at = lax.broadcasted_iota(jnp.int32, shape, axis)
        total = jnp.zeros(shape, jnp.int32)
        for edge in range(1, group_blocks):
            total = total + (at >= edge * block).astype(jnp.int32)
        return total

    square = (group, group)
    earlier = lax.broadcasted_iota(jnp.int32, square, 0) < lax.broadcasted_iota(jnp.int32, square, 1)
    if group_blocks > 1:
        earlier = earlier & (block_of(0, square) == block_of(1, square))
    earlier = earlier.astype(F32).astype(BF16)

    loads[0].wait()

    def make_order(which, carry):
        owner = owner_ref[which]
        owned = lax.broadcasted_iota(jnp.int32, (stations, group), 0) == owner
        ahead = jnp.dot(owned.astype(F32).astype(BF16), earlier, preferred_element_type=F32)
        rank = jnp.sum(jnp.where(owned, ahead, 0.0), axis=0, keepdims=True).astype(jnp.int32)
        slot = (block_of(1, (1, group)) * stations + owner) * rows + rank
        order = lax.broadcasted_iota(jnp.int32, (group_targets * rows, group), 0) == slot
        orders[which] = order.astype(F32).astype(BF16)
        return carry

    lax.fori_loop(0, groups, make_order, 0)

    loads[1].wait()
    few = 4

    chunks = length // LANES
    share = beams * inputs // few // chunks

    def widen(step):
        beam, at = lax.div(step, inputs // few), lax.rem(step, inputs // few)
        part = weights[beam, pl.ds(at * few, few)].astype(F32).reshape(2 * few, groups * group)
        for which in range(groups):
            wide[which, pl.ds(step * 2 * few, 2 * few), :] = part[:, which * group : (which + 1) * group]

    loads[2].wait()
    loads[3].wait()

    def filter_chunk(chunk, carry):
        at = pl.multiple_of(chunk * LANES, LANES)
        for step in range(share):
            widen(chunk * share + step)
        sums = [None] * frames
        for segment in range(frames + taps - 1):
            lanes = pl.ds(pl.multiple_of(segment * length + at, LANES), LANES)
            part = volts[:, lanes].astype(F32)
            for frame in range(frames):
                tap = segment - frame
                if 0 <= tap < taps:
                    term = taper_ref[tap : tap + 1, pl.ds(at, LANES)] * part
                    sums[frame] = term if sums[frame] is None else sums[frame] + term
        for frame in range(frames):
            filtered[frame * inputs : (frame + 1) * inputs, pl.ds(at, LANES)] = sums[frame].astype(BF16)
        return carry

    lax.fori_loop(0, chunks, filter_chunk, 0)

    loads[4].wait()
    beam_row = lax.broadcasted_iota(jnp.int32, (beams, group), 0)
    first = jnp.zeros((beams, group), jnp.int32)
    for beam in range(beams):
        first = jnp.where(beam_row == beam, starts_ref[beam], first)
    offset = sec - first
    offset = jnp.where(offset < 0, offset + sections, offset)
    inside = (offset < max(1, sections // 2)).astype(F32)

    def transform(step):
        target = (spectra_a, spectra_b)[step % 2]
        target[...] = jnp.dot(filtered[...], table[turns[step]], preferred_element_type=F32)

    loads[5].wait()
    transform(0)
    pl.semaphore_wait(barrier, devices - 1)

    for step in range(groups):
        which = turns[step]
        spectra = (spectra_a, spectra_b)[step % 2]
        if step + 1 < groups:
            loads[6 + step].wait()
            transform(step + 1)
        total = [[[None] * frames for _ in range(2)] for _ in range(2)]
        for entry in range(inputs):
            weight_r = wide[which, pl.ds(2 * entry, beams, stride=2 * inputs), :]
            weight_i = wide[which, pl.ds(2 * entry + 1, beams, stride=2 * inputs), :]
            mine = total[entry % 2]
            for frame in range(frames):
                row = frame * inputs + entry
                real = spectra[row : row + 1, :group]
                imag = spectra[row : row + 1, group:]
                sum_r = weight_r * real - weight_i * imag
                sum_i = weight_r * imag + weight_i * real
                mine[0][frame] = sum_r if mine[0][frame] is None else mine[0][frame] + sum_r
                mine[1][frame] = sum_i if mine[1][frame] is None else mine[1][frame] + sum_i
        shares = jnp.concatenate(
            [total[p][part][f] * inside for p in range(2) for part in range(2) for f in range(frames)],
            axis=0,
        ).astype(BF16)
        ordered = lax.dot_general(
            orders[which], shares, (((1,), (1,)), ((), ())), preferred_element_type=F32
        )
        base = which * group_targets
        outgoing[pl.ds(base, group_targets)] = ordered.astype(BF16).reshape(group_targets, rows, LANES)

        def send(turn, carry, last=step == groups - 1, which=which, base=base):
            part, turn = lax.div(turn, stations), lax.rem(turn, stations)
            to_st = lax.rem(st + turn, stations)
            target = base + part * stations + to_st

            def start():
                pltpu.make_async_remote_copy(
                    src_ref=outgoing.at[target], dst_ref=arrived.at[me],
                    send_sem=send_sem, recv_sem=recv_sem,
                    device_id=(to_st, which * group_blocks + part), device_id_type=MESH,
                ).start()

            if last:
                pl.when(target != me)(start)
            else:
                start()
            return carry

        lax.fori_loop(0, group_targets, send, 0, unroll=math.gcd(8, group_targets))

    arrived[me] = outgoing[me]
    others = pl.ds(0, devices - 1)
    pltpu.make_async_copy(arrived.at[others], arrived.at[others], recv_sem).wait()
    summed = arrived[0:stations].astype(F32)
    for other in range(1, sections):
        summed = summed + arrived[other * stations : (other + 1) * stations].astype(F32)
    out_ref[...] = summed.astype(BF16).reshape(stations * rows, LANES)
    pltpu.make_async_copy(outgoing.at[others], outgoing.at[others], send_sem).wait()


def correlate_kernel(
    dims, beams_hbm, place_hbm, out_hbm, beams_ref, place_ref, left, right, mask, result, sems, sem
):
    beams, frames, per_owner, signals = dims
    half = frames * beams
    loads = [
        pltpu.make_async_copy(beams_hbm, beams_ref, sems.at[0]),
        pltpu.make_async_copy(place_hbm, place_ref, sems.at[1]),
    ]
    for load in loads:
        load.start()
    full = (beams, frames, signals, LANES)
    column = lax.broadcasted_iota(jnp.int32, full, 1) * beams + lax.broadcasted_iota(jnp.int32, full, 0)
    lane = lax.broadcasted_iota(jnp.int32, full, 3)
    hit = (lane == column) | (lane == column + half)
    mask[...] = hit.astype(F32).astype(BF16).reshape(half, signals, LANES)
    for load in loads:
        load.wait()
    spread = jnp.dot(place_ref[...], beams_ref[...], preferred_element_type=F32)
    shape = spread.shape
    lane = lax.broadcasted_iota(jnp.int32, shape, 1)
    odd = (lax.broadcasted_iota(jnp.int32, shape, 0) & 1) == 1
    both = jnp.where(odd, pltpu.roll(spread, 2 * half, 1), spread)
    turned = jnp.where(lane < half, -pltpu.roll(both, LANES - half, 1), pltpu.roll(both, half, 1))
    left[...] = both.astype(BF16).reshape(per_owner, signals, LANES)
    right[:, :signals] = left[...]
    right[:, signals:] = turned.astype(BF16).reshape(per_owner, signals, LANES)

    batch = math.gcd(4, per_owner)

    def channels(step, carry):
        first = step * batch
        products = []
        for at in range(batch):
            masked = (left[first + at][None] * mask[...]).reshape(half * signals, LANES)
            products.append(
                lax.dot_general(
                    masked, right[first + at], (((1,), (1,)), ((), ())), preferred_element_type=F32
                )
            )
        for at in range(batch):
            result[first + at] = products[at].astype(BF16).reshape(beams, frames, signals, 2 * signals)
        several = pl.ds(first, batch)
        pltpu.make_async_copy(result.at[several], out_hbm.at[0, 0, several], sem).start()
        return carry

    lax.fori_loop(0, per_owner // batch, channels, 0, unroll=True)
    pltpu.make_async_copy(result, out_hbm.at[0, 0], sem).wait()


def local(voltages, taper, beam_weight_table, starts, owner_map):
    inputs = voltages.shape[1]
    taps, length = taper.shape
    frames = voltages.shape[2] // length - taps + 1
    channels = length // 2
    beams = beam_weight_table.shape[1]
    sections = lax.axis_size("section")
    stations = lax.axis_size("station")
    block = channels // sections
    per_owner = block // stations
    group = max(LANES, block)
    groups = channels // group
    rows = -(-per_owner // 16) * 16
    devices = sections * stations
    signals = 2 * stations
    values = 4 * frames * beams
    dims = (sections, stations, inputs, frames, taps, length, beams, group, block, per_owner, rows)

    table = jnp.asarray(dft_table(length, group))
    owners = owner_map.reshape(groups, 1, group)
    vmem = pl.BlockSpec(memory_space=pltpu.VMEM)
    hbm = pl.BlockSpec(memory_space=pl.ANY)
    mine = pl.pallas_call(
        functools.partial(beam_kernel, dims),
        out_shape=jax.ShapeDtypeStruct((stations * rows, values), BF16),
        in_specs=[hbm] * 6,
        out_specs=vmem,
        scratch_shapes=[
            pltpu.SMEM(starts.shape, jnp.int32),
            pltpu.VMEM(owners.shape, jnp.int32),
            pltpu.VMEM(taper.shape, F32),
            pltpu.VMEM(voltages.shape[1:], BF16),
            pltpu.VMEM(beam_weight_table.shape[1:], BF16),
            pltpu.VMEM((groups, 2 * beams * inputs, group), F32),
            pltpu.VMEM(table.shape, BF16),
            pltpu.VMEM((frames * inputs, length), BF16),
            pltpu.VMEM((frames * inputs, 2 * group), F32),
            pltpu.VMEM((frames * inputs, 2 * group), F32),
            pltpu.VMEM((groups, group // per_owner * rows, group), BF16),
            pltpu.VMEM((devices, rows, values), BF16),
            pltpu.VMEM((devices, rows, values), BF16),
            pltpu.SemaphoreType.DMA((5 + groups,)),
            pltpu.SemaphoreType.DMA,
            pltpu.SemaphoreType.DMA,
        ],
        compiler_params=pltpu.CompilerParams(
            collective_id=0, has_side_effects=True, vmem_limit_bytes=VMEM_LIMIT
        ),
    )(starts, owners, taper, voltages, beam_weight_table, table)

    place = np.zeros((per_owner, stations, 2, stations, rows), np.float32)
    for at in range(per_owner):
        for station in range(stations):
            place[at, station, :, station, at] = 1.0
    place = jnp.asarray(place.reshape(per_owner * signals, stations * rows).astype(jnp.bfloat16))
    return pl.pallas_call(
        functools.partial(correlate_kernel, (beams, frames, per_owner, signals)),
        out_shape=jax.ShapeDtypeStruct(
            (1, 1, per_owner, beams, frames, signals, 2 * signals), BF16
        ),
        in_specs=[hbm, hbm],
        out_specs=hbm,
        scratch_shapes=[
            pltpu.VMEM(mine.shape, BF16),
            pltpu.VMEM(place.shape, BF16),
            pltpu.VMEM((per_owner, signals, LANES), BF16),
            pltpu.VMEM((per_owner, 2 * signals, LANES), BF16),
            pltpu.VMEM((frames * beams, signals, LANES), BF16),
            pltpu.VMEM((per_owner, beams, frames, signals, 2 * signals), BF16),
            pltpu.SemaphoreType.DMA((2,)),
            pltpu.SemaphoreType.DMA,
        ],
        compiler_params=pltpu.CompilerParams(vmem_limit_bytes=VMEM_LIMIT),
    )(mine, place)


def solution(mesh):
    placed = (
        P("station", "section", None),
        P(),
        P("station", None, "section", None, None),
        P(),
        P(),
    )
    return jax.shard_map(
        local,
        mesh=mesh,
        in_specs=placed,
        out_specs=P("section", "station", None, None, None, None, None),
        check_vma=False,
    )
```

```python
import functools
import math

import jax
import jax.numpy as jnp
import numpy as np
from jax import lax
from jax.experimental import pallas as pl
from jax.experimental.pallas import tpu as pltpu
from jax.sharding import PartitionSpec as P

MESH = pl.DeviceIdType.MESH
LANES = 128
VMEM_LIMIT = 60 * 1024 * 1024
F32 = jnp.float32
BF16 = jnp.bfloat16


def dft_table(length, group):
    half = length // 2
    index_n = np.arange(length, dtype=np.int64)[:, None]
    index_k = np.arange(half, dtype=np.int64)[None, :]
    phase = (index_n * index_k % length).astype(np.float32) * np.float32(2.0 * math.pi / length)
    factor = np.float32(1.0 / math.sqrt(length))
    real = (np.cos(phase) * factor).reshape(length, half // group, group)
    imag = (-np.sin(phase) * factor).reshape(length, half // group, group)
    return np.concatenate([real, imag], axis=2).transpose(1, 0, 2).astype(jnp.bfloat16)


def beam_kernel(
    dims, starts_hbm, owner_hbm, taper_hbm, volts_hbm, weights_hbm, table_hbm, out_ref,
    starts_ref, owner_ref, taper_ref, volts, weights, wide, table, filtered, spectra_a, spectra_b, orders,
    outgoing, arrived, load_sems, send_sem, recv_sem,
):
    sections, stations, inputs, frames, taps, length, beams, group, block, per_owner, rows = dims
    st = lax.axis_index("station")
    sec = lax.axis_index("section")
    devices = sections * stations
    me = sec * stations + st
    groups = table.shape[0]
    group_blocks = group // block
    group_targets = group_blocks * stations

    own_group = lax.div(sec, group_blocks)
    turns = [lax.rem(own_group + 1 + step, groups) for step in range(groups)]
    pairs = [
        (owner_hbm, owner_ref), (weights_hbm.at[0], weights), (volts_hbm.at[0], volts),
        (taper_hbm, taper_ref), (starts_hbm, starts_ref),
    ]
    pairs += [(table_hbm.at[turn], table.at[turn]) for turn in turns]
    loads = [
        pltpu.make_async_copy(here, there, load_sems.at[at]) for at, (here, there) in enumerate(pairs)
    ]
    for load in loads:
        load.start()

    barrier = pltpu.get_barrier_semaphore()

    def greet(step, carry):
        other = lax.rem(me + step, devices)
        pl.semaphore_signal(
            barrier, inc=1, device_id=(lax.rem(other, stations), lax.div(other, stations)),
            device_id_type=MESH,
        )
        return carry

    lax.fori_loop(1, devices, greet, 0)

    def block_of(axis, shape):
        at = lax.broadcasted_iota(jnp.int32, shape, axis)
        total = jnp.zeros(shape, jnp.int32)
        for edge in range(1, group_blocks):
            total = total + (at >= edge * block).astype(jnp.int32)
        return total

    square = (group, group)
    earlier = lax.broadcasted_iota(jnp.int32, square, 0) < lax.broadcasted_iota(jnp.int32, square, 1)
    if group_blocks > 1:
        earlier = earlier & (block_of(0, square) == block_of(1, square))
    earlier = earlier.astype(F32).astype(BF16)

    loads[0].wait()

    def make_order(which, carry):
        owner = owner_ref[which]
        owned = lax.broadcasted_iota(jnp.int32, (stations, group), 0) == owner
        ahead = jnp.dot(owned.astype(F32).astype(BF16), earlier, preferred_element_type=F32)
        rank = jnp.sum(jnp.where(owned, ahead, 0.0), axis=0, keepdims=True).astype(jnp.int32)
        slot = (block_of(1, (1, group)) * stations + owner) * rows + rank
        order = lax.broadcasted_iota(jnp.int32, (group_targets * rows, group), 0) == slot
        orders[which] = order.astype(F32).astype(BF16)
        return carry

    lax.fori_loop(0, groups, make_order, 0)

    loads[1].wait()
    few = 4

    chunks = length // LANES
    share = beams * inputs // few // chunks

    def widen(step):
        beam, at = lax.div(step, inputs // few), lax.rem(step, inputs // few)
        part = weights[beam, pl.ds(at * few, few)].astype(F32).reshape(2 * few, groups * group)
        for which in range(groups):
            wide[which, pl.ds(step * 2 * few, 2 * few), :] = part[:, which * group : (which + 1) * group]

    loads[2].wait()
    loads[3].wait()

    def filter_chunk(chunk, carry):
        at = pl.multiple_of(chunk * LANES, LANES)
        for step in range(share):
            widen(chunk * share + step)
        sums = [None] * frames
        for segment in range(frames + taps - 1):
            lanes = pl.ds(pl.multiple_of(segment * length + at, LANES), LANES)
            part = volts[:, lanes].astype(F32)
            for frame in range(frames):
                tap = segment - frame
                if 0 <= tap < taps:
                    term = taper_ref[tap : tap + 1, pl.ds(at, LANES)] * part
                    sums[frame] = term if sums[frame] is None else sums[frame] + term
        for frame in range(frames):
            filtered[frame * inputs : (frame + 1) * inputs, pl.ds(at, LANES)] = sums[frame].astype(BF16)
        return carry

    lax.fori_loop(0, chunks, filter_chunk, 0)

    loads[4].wait()
    beam_row = lax.broadcasted_iota(jnp.int32, (beams, group), 0)
    first = jnp.zeros((beams, group), jnp.int32)
    for beam in range(beams):
        first = jnp.where(beam_row == beam, starts_ref[beam], first)
    offset = sec - first
    offset = jnp.where(offset < 0, offset + sections, offset)
    inside = (offset < max(1, sections // 2)).astype(F32)

    def transform(step):
        target = (spectra_a, spectra_b)[step % 2]
        target[...] = jnp.dot(filtered[...], table[turns[step]], preferred_element_type=F32)

    loads[5].wait()
    transform(0)

    for step in range(groups):
        which = turns[step]
        spectra = (spectra_a, spectra_b)[step % 2]
        if step + 1 < groups:
            loads[6 + step].wait()
            transform(step + 1)
        total = [[[None] * frames for _ in range(2)] for _ in range(2)]
        for entry in range(inputs):
            weight_r = wide[which, pl.ds(2 * entry, beams, stride=2 * inputs), :]
            weight_i = wide[which, pl.ds(2 * entry + 1, beams, stride=2 * inputs), :]
            mine = total[entry % 2]
            for frame in range(frames):
                row = frame * inputs + entry
                real = spectra[row : row + 1, :group]
                imag = spectra[row : row + 1, group:]
                sum_r = weight_r * real - weight_i * imag
                sum_i = weight_r * imag + weight_i * real
                mine[0][frame] = sum_r if mine[0][frame] is None else mine[0][frame] + sum_r
                mine[1][frame] = sum_i if mine[1][frame] is None else mine[1][frame] + sum_i
        shares = jnp.concatenate(
            [total[p][part][f] * inside for p in range(2) for part in range(2) for f in range(frames)],
            axis=0,
        ).astype(BF16)
        ordered = lax.dot_general(
            orders[which], shares, (((1,), (1,)), ((), ())), preferred_element_type=F32
        )
        base = which * group_targets
        outgoing[pl.ds(base, group_targets)] = ordered.astype(BF16).reshape(group_targets, rows, LANES)

        if step == 0:
            pl.semaphore_wait(barrier, devices - 1)

        def send(turn, carry, last=step == groups - 1, which=which, base=base):
            part, turn = lax.div(turn, stations), lax.rem(turn, stations)
            to_st = lax.rem(st + turn, stations)
            target = base + part * stations + to_st

            def start():
                pltpu.make_async_remote_copy(
                    src_ref=outgoing.at[target], dst_ref=arrived.at[me],
                    send_sem=send_sem, recv_sem=recv_sem,
                    device_id=(to_st, which * group_blocks + part), device_id_type=MESH,
                ).start()

            if last:
                pl.when(target != me)(start)
            else:
                start()
            return carry

        lax.fori_loop(0, group_targets, send, 0, unroll=math.gcd(8, group_targets))

    arrived[me] = outgoing[me]
    others = pl.ds(0, devices - 1)
    pltpu.make_async_copy(arrived.at[others], arrived.at[others], recv_sem).wait()
    summed = arrived[0:stations].astype(F32)
    for other in range(1, sections):
        summed = summed + arrived[other * stations : (other + 1) * stations].astype(F32)
    out_ref[...] = summed.astype(BF16).reshape(stations * rows, LANES)
    pltpu.make_async_copy(outgoing.at[others], outgoing.at[others], send_sem).wait()


def correlate_kernel(
    dims, beams_hbm, place_hbm, out_hbm, beams_ref, place_ref, left, right, mask, result, sems, sem
):
    beams, frames, per_owner, signals = dims
    half = frames * beams
    loads = [
        pltpu.make_async_copy(beams_hbm, beams_ref, sems.at[0]),
        pltpu.make_async_copy(place_hbm, place_ref, sems.at[1]),
    ]
    for load in loads:
        load.start()
    full = (beams, frames, signals, LANES)
    column = lax.broadcasted_iota(jnp.int32, full, 1) * beams + lax.broadcasted_iota(jnp.int32, full, 0)
    lane = lax.broadcasted_iota(jnp.int32, full, 3)
    hit = (lane == column) | (lane == column + half)
    mask[...] = hit.astype(F32).astype(BF16).reshape(half, signals, LANES)
    for load in loads:
        load.wait()
    spread = jnp.dot(place_ref[...], beams_ref[...], preferred_element_type=F32)
    shape = spread.shape
    lane = lax.broadcasted_iota(jnp.int32, shape, 1)
    odd = (lax.broadcasted_iota(jnp.int32, shape, 0) & 1) == 1
    both = jnp.where(odd, pltpu.roll(spread, 2 * half, 1), spread)
    turned = jnp.where(lane < half, -pltpu.roll(both, LANES - half, 1), pltpu.roll(both, half, 1))
    left[...] = both.astype(BF16).reshape(per_owner, signals, LANES)
    right[:, :signals] = left[...]
    right[:, signals:] = turned.astype(BF16).reshape(per_owner, signals, LANES)

    batch = math.gcd(4, per_owner)

    def channels(step, carry):
        first = step * batch
        products = []
        for at in range(batch):
            masked = (left[first + at][None] * mask[...]).reshape(half * signals, LANES)
            products.append(
                lax.dot_general(
                    masked, right[first + at], (((1,), (1,)), ((), ())), preferred_element_type=F32
                )
            )
        for at in range(batch):
            result[first + at] = products[at].astype(BF16).reshape(beams, frames, signals, 2 * signals)
        several = pl.ds(first, batch)
        pltpu.make_async_copy(result.at[several], out_hbm.at[0, 0, several], sem).start()
        return carry

    lax.fori_loop(0, per_owner // batch, channels, 0, unroll=True)
    pltpu.make_async_copy(result, out_hbm.at[0, 0], sem).wait()


def local(voltages, taper, beam_weight_table, starts, owner_map):
    inputs = voltages.shape[1]
    taps, length = taper.shape
    frames = voltages.shape[2] // length - taps + 1
    channels = length // 2
    beams = beam_weight_table.shape[1]
    sections = lax.axis_size("section")
    stations = lax.axis_size("station")
    block = channels // sections
    per_owner = block // stations
    group = max(LANES, block)
    groups = channels // group
    rows = -(-per_owner // 16) * 16
    devices = sections * stations
    signals = 2 * stations
    values = 4 * frames * beams
    dims = (sections, stations, inputs, frames, taps, length, beams, group, block, per_owner, rows)

    table = jnp.asarray(dft_table(length, group))
    owners = owner_map.reshape(groups, 1, group)
    vmem = pl.BlockSpec(memory_space=pltpu.VMEM)
    hbm = pl.BlockSpec(memory_space=pl.ANY)
    mine = pl.pallas_call(
        functools.partial(beam_kernel, dims),
        out_shape=jax.ShapeDtypeStruct((stations * rows, values), BF16),
        in_specs=[hbm] * 6,
        out_specs=vmem,
        scratch_shapes=[
            pltpu.SMEM(starts.shape, jnp.int32),
            pltpu.VMEM(owners.shape, jnp.int32),
            pltpu.VMEM(taper.shape, F32),
            pltpu.VMEM(voltages.shape[1:], BF16),
            pltpu.VMEM(beam_weight_table.shape[1:], BF16),
            pltpu.VMEM((groups, 2 * beams * inputs, group), F32),
            pltpu.VMEM(table.shape, BF16),
            pltpu.VMEM((frames * inputs, length), BF16),
            pltpu.VMEM((frames * inputs, 2 * group), F32),
            pltpu.VMEM((frames * inputs, 2 * group), F32),
            pltpu.VMEM((groups, group // per_owner * rows, group), BF16),
            pltpu.VMEM((devices, rows, values), BF16),
            pltpu.VMEM((devices, rows, values), BF16),
            pltpu.SemaphoreType.DMA((5 + groups,)),
            pltpu.SemaphoreType.DMA,
            pltpu.SemaphoreType.DMA,
        ],
        compiler_params=pltpu.CompilerParams(
            collective_id=0, has_side_effects=True, vmem_limit_bytes=VMEM_LIMIT
        ),
    )(starts, owners, taper, voltages, beam_weight_table, table)

    place = np.zeros((per_owner, stations, 2, stations, rows), np.float32)
    for at in range(per_owner):
        for station in range(stations):
            place[at, station, :, station, at] = 1.0
    place = jnp.asarray(place.reshape(per_owner * signals, stations * rows).astype(jnp.bfloat16))
    return pl.pallas_call(
        functools.partial(correlate_kernel, (beams, frames, per_owner, signals)),
        out_shape=jax.ShapeDtypeStruct(
            (1, 1, per_owner, beams, frames, signals, 2 * signals), BF16
        ),
        in_specs=[hbm, hbm],
        out_specs=hbm,
        scratch_shapes=[
            pltpu.VMEM(mine.shape, BF16),
            pltpu.VMEM(place.shape, BF16),
            pltpu.VMEM((per_owner, signals, LANES), BF16),
            pltpu.VMEM((per_owner, 2 * signals, LANES), BF16),
            pltpu.VMEM((frames * beams, signals, LANES), BF16),
            pltpu.VMEM((per_owner, beams, frames, signals, 2 * signals), BF16),
            pltpu.SemaphoreType.DMA((2,)),
            pltpu.SemaphoreType.DMA,
        ],
        compiler_params=pltpu.CompilerParams(vmem_limit_bytes=VMEM_LIMIT),
    )(mine, place)


def solution(mesh):
    placed = (
        P("station", "section", None),
        P(),
        P("station", None, "section", None, None),
        P(),
        P(),
    )
    return jax.shard_map(
        local,
        mesh=mesh,
        in_specs=placed,
        out_specs=P("section", "station", None, None, None, None, None),
        check_vma=False,
    )
```

```python
import functools
import math

import jax
import jax.numpy as jnp
import numpy as np
from jax import lax
from jax.experimental import pallas as pl
from jax.experimental.pallas import tpu as pltpu
from jax.sharding import PartitionSpec as P

MESH = pl.DeviceIdType.MESH
LANES = 128
VMEM_LIMIT = 60 * 1024 * 1024
F32 = jnp.float32
BF16 = jnp.bfloat16


def dft_table(length, group):
    half = length // 2
    index_n = np.arange(length, dtype=np.int64)[:, None]
    index_k = np.arange(half, dtype=np.int64)[None, :]
    phase = (index_n * index_k % length).astype(np.float32) * np.float32(2.0 * math.pi / length)
    factor = np.float32(1.0 / math.sqrt(length))
    real = (np.cos(phase) * factor).reshape(length, half // group, group)
    imag = (-np.sin(phase) * factor).reshape(length, half // group, group)
    return np.concatenate([real, imag], axis=2).transpose(1, 0, 2).astype(jnp.bfloat16)


def beam_kernel(
    dims, starts_hbm, owner_hbm, taper_hbm, volts_hbm, weights_hbm, table_hbm, out_ref,
    starts_ref, owner_ref, taper_ref, volts, weights, wide, table, filtered, spectra_a, spectra_b, orders,
    outgoing, arrived, load_sems, send_sem, recv_sem,
):
    sections, stations, inputs, frames, taps, length, beams, group, block, per_owner, rows = dims
    st = lax.axis_index("station")
    sec = lax.axis_index("section")
    devices = sections * stations
    me = sec * stations + st
    groups = table.shape[0]
    group_blocks = group // block
    group_targets = group_blocks * stations

    own_group = lax.div(sec, group_blocks)
    turns = [lax.rem(own_group + 1 + step, groups) for step in range(groups)]
    pairs = [
        (owner_hbm, owner_ref), (weights_hbm.at[0], weights), (volts_hbm.at[0], volts),
        (taper_hbm, taper_ref), (starts_hbm, starts_ref),
    ]
    pairs += [(table_hbm.at[turn], table.at[turn]) for turn in turns]
    loads = [
        pltpu.make_async_copy(here, there, load_sems.at[at]) for at, (here, there) in enumerate(pairs)
    ]
    for load in loads:
        load.start()

    barrier = pltpu.get_barrier_semaphore()

    def greet(step, carry):
        other = lax.rem(me + step, devices)
        pl.semaphore_signal(
            barrier, inc=1, device_id=(lax.rem(other, stations), lax.div(other, stations)),
            device_id_type=MESH,
        )
        return carry

    lax.fori_loop(1, devices, greet, 0)

    def block_of(axis, shape):
        at = lax.broadcasted_iota(jnp.int32, shape, axis)
        total = jnp.zeros(shape, jnp.int32)
        for edge in range(1, group_blocks):
            total = total + (at >= edge * block).astype(jnp.int32)
        return total

    square = (group, group)
    earlier = lax.broadcasted_iota(jnp.int32, square, 0) < lax.broadcasted_iota(jnp.int32, square, 1)
    if group_blocks > 1:
        earlier = earlier & (block_of(0, square) == block_of(1, square))
    earlier = earlier.astype(F32).astype(BF16)

    loads[0].wait()

    def make_order(which, carry):
        owner = owner_ref[which]
        owned = lax.broadcasted_iota(jnp.int32, (stations, group), 0) == owner
        ahead = jnp.dot(owned.astype(F32).astype(BF16), earlier, preferred_element_type=F32)
        rank = jnp.sum(jnp.where(owned, ahead, 0.0), axis=0, keepdims=True).astype(jnp.int32)
        slot = (block_of(1, (1, group)) * stations + owner) * rows + rank
        order = lax.broadcasted_iota(jnp.int32, (group_targets * rows, group), 0) == slot
        orders[which] = order.astype(F32).astype(BF16)
        return carry

    lax.fori_loop(0, groups, make_order, 0)

    loads[1].wait()
    few = 4

    chunks = length // LANES
    share = beams * inputs // few // chunks

    def widen(step):
        beam, at = lax.div(step, inputs // few), lax.rem(step, inputs // few)
        part = weights[beam, pl.ds(at * few, few)].astype(F32).reshape(2 * few, groups * group)
        for which in range(groups):
            wide[which, pl.ds(step * 2 * few, 2 * few), :] = part[:, which * group : (which + 1) * group]

    loads[2].wait()
    loads[3].wait()

    def filter_chunk(chunk, carry):
        at = pl.multiple_of(chunk * LANES, LANES)
        for step in range(share):
            widen(chunk * share + step)
        sums = [None] * frames
        for segment in range(frames + taps - 1):
            lanes = pl.ds(pl.multiple_of(segment * length + at, LANES), LANES)
            part = volts[:, lanes].astype(F32)
            for frame in range(frames):
                tap = segment - frame
                if 0 <= tap < taps:
                    term = taper_ref[tap : tap + 1, pl.ds(at, LANES)] * part
                    sums[frame] = term if sums[frame] is None else sums[frame] + term
        for frame in range(frames):
            filtered[frame * inputs : (frame + 1) * inputs, pl.ds(at, LANES)] = sums[frame].astype(BF16)
        return carry

    lax.fori_loop(0, chunks, filter_chunk, 0)

    loads[4].wait()
    beam_row = lax.broadcasted_iota(jnp.int32, (beams, group), 0)
    first = jnp.zeros((beams, group), jnp.int32)
    for beam in range(beams):
        first = jnp.where(beam_row == beam, starts_ref[beam], first)
    offset = sec - first
    offset = jnp.where(offset < 0, offset + sections, offset)
    inside = (offset < max(1, sections // 2)).astype(F32)

    def transform(step):
        target = (spectra_a, spectra_b)[step % 2]
        target[...] = jnp.dot(filtered[...], table[turns[step]], preferred_element_type=F32)

    loads[5].wait()
    transform(0)

    for step in range(groups):
        which = turns[step]
        spectra = (spectra_a, spectra_b)[step % 2]
        if step + 1 < groups:
            loads[6 + step].wait()
            transform(step + 1)
        total = [[[None] * frames for _ in range(2)] for _ in range(2)]
        for entry in range(inputs):
            weight_r = wide[which, pl.ds(2 * entry, beams, stride=2 * inputs), :]
            weight_i = wide[which, pl.ds(2 * entry + 1, beams, stride=2 * inputs), :]
            mine = total[entry % 2]
            for frame in range(frames):
                row = frame * inputs + entry
                real = spectra[row : row + 1, :group]
                imag = spectra[row : row + 1, group:]
                sum_r = weight_r * real - weight_i * imag
                sum_i = weight_r * imag + weight_i * real
                mine[0][frame] = sum_r if mine[0][frame] is None else mine[0][frame] + sum_r
                mine[1][frame] = sum_i if mine[1][frame] is None else mine[1][frame] + sum_i
        shares = jnp.concatenate(
            [total[p][part][f] * inside for p in range(2) for part in range(2) for f in range(frames)],
            axis=0,
        ).astype(BF16)
        ordered = lax.dot_general(
            orders[which], shares, (((1,), (1,)), ((), ())), preferred_element_type=F32
        )
        base = which * group_targets
        outgoing[pl.ds(base, group_targets)] = ordered.astype(BF16).reshape(group_targets, rows, LANES)

        if step == 0:
            pl.semaphore_wait(barrier, devices - 1)

        def send(turn, carry, last=step == groups - 1, which=which, base=base):
            part, turn = lax.div(turn, stations), lax.rem(turn, stations)
            to_st = lax.rem(st + turn, stations)
            target = base + part * stations + to_st

            def start():
                pltpu.make_async_remote_copy(
                    src_ref=outgoing.at[target], dst_ref=arrived.at[me],
                    send_sem=send_sem, recv_sem=recv_sem,
                    device_id=(to_st, which * group_blocks + part), device_id_type=MESH,
                ).start()

            if last:
                pl.when(target != me)(start)
            else:
                start()
            return carry

        lax.fori_loop(0, group_targets, send, 0, unroll=math.gcd(8, group_targets))

    arrived[me] = outgoing[me]
    others = pl.ds(0, devices - 1)
    pltpu.make_async_copy(arrived.at[others], arrived.at[others], recv_sem).wait()
    summed = arrived[0:stations].astype(F32)
    for other in range(1, sections):
        summed = summed + arrived[other * stations : (other + 1) * stations].astype(F32)
    out_ref[...] = summed.astype(BF16).reshape(stations * rows, LANES)
    pltpu.make_async_copy(outgoing.at[others], outgoing.at[others], send_sem).wait()


def correlate_kernel(
    dims, beams_hbm, place_hbm, out_hbm, beams_ref, place_ref, left, right, mask, result, sems, sem
):
    beams, frames, per_owner, signals = dims
    half = frames * beams
    loads = [
        pltpu.make_async_copy(beams_hbm, beams_ref, sems.at[0]),
        pltpu.make_async_copy(place_hbm, place_ref, sems.at[1]),
    ]
    for load in loads:
        load.start()
    full = (beams, frames, signals, LANES)
    column = lax.broadcasted_iota(jnp.int32, full, 1) * beams + lax.broadcasted_iota(jnp.int32, full, 0)
    lane = lax.broadcasted_iota(jnp.int32, full, 3)
    hit = (lane == column) | (lane == column + half)
    mask[...] = hit.astype(F32).astype(BF16).reshape(half, signals, LANES)
    for load in loads:
        load.wait()
    spread = jnp.dot(place_ref[...], beams_ref[...], preferred_element_type=F32)
    shape = spread.shape
    lane = lax.broadcasted_iota(jnp.int32, shape, 1)
    odd = (lax.broadcasted_iota(jnp.int32, shape, 0) & 1) == 1
    both = jnp.where(odd, pltpu.roll(spread, 2 * half, 1), spread)
    turned = jnp.where(lane < half, -pltpu.roll(both, LANES - half, 1), pltpu.roll(both, half, 1))
    left[...] = both.astype(BF16).reshape(per_owner, signals, LANES)
    right[:, :signals] = left[...]
    right[:, signals:] = turned.astype(BF16).reshape(per_owner, signals, LANES)

    batch = math.gcd(2, per_owner)

    def channels(step, carry):
        first = step * batch
        products = []
        for at in range(batch):
            masked = (left[first + at][None] * mask[...]).reshape(half * signals, LANES)
            products.append(
                lax.dot_general(
                    masked, right[first + at], (((1,), (1,)), ((), ())), preferred_element_type=F32
                )
            )
        for at in range(batch):
            result[first + at] = products[at].astype(BF16).reshape(beams, frames, signals, 2 * signals)
        several = pl.ds(first, batch)
        pltpu.make_async_copy(result.at[several], out_hbm.at[0, 0, several], sem).start()
        return carry

    lax.fori_loop(0, per_owner // batch, channels, 0, unroll=True)
    pltpu.make_async_copy(result, out_hbm.at[0, 0], sem).wait()


def local(voltages, taper, beam_weight_table, starts, owner_map):
    inputs = voltages.shape[1]
    taps, length = taper.shape
    frames = voltages.shape[2] // length - taps + 1
    channels = length // 2
    beams = beam_weight_table.shape[1]
    sections = lax.axis_size("section")
    stations = lax.axis_size("station")
    block = channels // sections
    per_owner = block // stations
    group = max(LANES, block)
    groups = channels // group
    rows = -(-per_owner // 16) * 16
    devices = sections * stations
    signals = 2 * stations
    values = 4 * frames * beams
    dims = (sections, stations, inputs, frames, taps, length, beams, group, block, per_owner, rows)

    table = jnp.asarray(dft_table(length, group))
    owners = owner_map.reshape(groups, 1, group)
    vmem = pl.BlockSpec(memory_space=pltpu.VMEM)
    hbm = pl.BlockSpec(memory_space=pl.ANY)
    mine = pl.pallas_call(
        functools.partial(beam_kernel, dims),
        out_shape=jax.ShapeDtypeStruct((stations * rows, values), BF16),
        in_specs=[hbm] * 6,
        out_specs=vmem,
        scratch_shapes=[
            pltpu.SMEM(starts.shape, jnp.int32),
            pltpu.VMEM(owners.shape, jnp.int32),
            pltpu.VMEM(taper.shape, F32),
            pltpu.VMEM(voltages.shape[1:], BF16),
            pltpu.VMEM(beam_weight_table.shape[1:], BF16),
            pltpu.VMEM((groups, 2 * beams * inputs, group), F32),
            pltpu.VMEM(table.shape, BF16),
            pltpu.VMEM((frames * inputs, length), BF16),
            pltpu.VMEM((frames * inputs, 2 * group), F32),
            pltpu.VMEM((frames * inputs, 2 * group), F32),
            pltpu.VMEM((groups, group // per_owner * rows, group), BF16),
            pltpu.VMEM((devices, rows, values), BF16),
            pltpu.VMEM((devices, rows, values), BF16),
            pltpu.SemaphoreType.DMA((5 + groups,)),
            pltpu.SemaphoreType.DMA,
            pltpu.SemaphoreType.DMA,
        ],
        compiler_params=pltpu.CompilerParams(
            collective_id=0, has_side_effects=True, vmem_limit_bytes=VMEM_LIMIT
        ),
    )(starts, owners, taper, voltages, beam_weight_table, table)

    place = np.zeros((per_owner, stations, 2, stations, rows), np.float32)
    for at in range(per_owner):
        for station in range(stations):
            place[at, station, :, station, at] = 1.0
    place = jnp.asarray(place.reshape(per_owner * signals, stations * rows).astype(jnp.bfloat16))
    return pl.pallas_call(
        functools.partial(correlate_kernel, (beams, frames, per_owner, signals)),
        out_shape=jax.ShapeDtypeStruct(
            (1, 1, per_owner, beams, frames, signals, 2 * signals), BF16
        ),
        in_specs=[hbm, hbm],
        out_specs=hbm,
        scratch_shapes=[
            pltpu.VMEM(mine.shape, BF16),
            pltpu.VMEM(place.shape, BF16),
            pltpu.VMEM((per_owner, signals, LANES), BF16),
            pltpu.VMEM((per_owner, 2 * signals, LANES), BF16),
            pltpu.VMEM((frames * beams, signals, LANES), BF16),
            pltpu.VMEM((per_owner, beams, frames, signals, 2 * signals), BF16),
            pltpu.SemaphoreType.DMA((2,)),
            pltpu.SemaphoreType.DMA,
        ],
        compiler_params=pltpu.CompilerParams(vmem_limit_bytes=VMEM_LIMIT),
    )(mine, place)


def solution(mesh):
    placed = (
        P("station", "section", None),
        P(),
        P("station", None, "section", None, None),
        P(),
        P(),
    )
    return jax.shard_map(
        local,
        mesh=mesh,
        in_specs=placed,
        out_specs=P("section", "station", None, None, None, None, None),
        check_vma=False,
    )
```
